512 devices in a mesh: ctx: 64 (over y, z), head: 8 (over x, core).
Axes of the slice: x: 4, y: 4, z: 16, core: 2. Of those that a mesh axis runs over, the one named last changes fastest.
Arguments:
- queries: bfloat16 [32768, 4096], P('ctx', 'head'), may hold values from -6 to 6
- keys: bfloat16 [32768, 4096], P('ctx', 'head'), may hold values from -6 to 6
- values: bfloat16 [32768, 4096], P('ctx', 'head'), may hold values from -6 to 6
- gain: float32 [4096], P('head'), may hold values from 0.1 to 1.9
- out_grad: bfloat16 [32768, 4096], P('ctx', 'head'), may hold values from -6 to 6
Outputs:
- normed: bfloat16 [32768, 4096], P('ctx', 'head')
- query_grad: bfloat16 [32768, 4096], P('ctx', 'head')
- key_grad: bfloat16 [32768, 4096], P('ctx', 'head')
- value_grad: bfloat16 [32768, 4096], P('ctx', 'head')
The draws below stay inside these ranges and needn't reach their ends.
All inputs are finite; a program needn't handle non-finite values.
Results may differ from the reference program's by a relative error of at most 0.0058.
Values sent between devices are 32-bit elements; how exact they have to be, the bound alone decides.
A program may use at most 64 MiB of HBM per device.

```python
import jax
import jax.numpy as jnp
from jax import lax

H = 32
HD = 128
BLOCK = 512
TOKENS = 32768
F = 4096


def shard_levels(rng, extent, split, least, top_value):
    loudness, own = 1.0, jax.random.fold_in(rng, 6)
    for dim, shards_of in split:
        steps = jnp.exp(jax.random.uniform(jax.random.fold_in(own, dim), (shards_of,), jnp.float32, least / len(split), top_value / len(split)))
        loudness = loudness * jnp.repeat(steps, extent[dim] // shards_of).reshape([-1 if axis == dim else 1 for axis in range(len(extent))])
    return loudness


def bell_draw(stream_key, shape, width, reach, cuts=(), kind=jnp.bfloat16):
    values = width * jax.random.normal(stream_key, shape, jnp.float32)
    if cuts:
        values = values * shard_levels(stream_key, shape, cuts, -0.22, 0.18)
    return jnp.clip(values, -reach, reach).astype(kind)


def setup_inputs(seed: int = 0) -> dict:
    key_of = jax.random.split(jax.random.key(seed), 6)
    return {
        "queries": bell_draw(key_of[0], (TOKENS, F), 1.0, 6.0, ((0, 64), (1, 8))),
        "keys": bell_draw(key_of[1], (TOKENS, F), 1.0, 6.0, ((0, 64), (1, 8))),
        "values": bell_draw(key_of[2], (TOKENS, F), 1.0, 6.0, ((0, 64), (1, 8))),
        "gain": jnp.clip(1.0 + 0.18 * jax.random.normal(key_of[3], (F,), jnp.float32), 0.1, 1.9),
        "out_grad": bell_draw(key_of[4], (TOKENS, F), 1.0, 6.0, ((0, 64), (1, 8))),
    }


def round_half(x):
    low = lax.optimization_barrier(x.astype(jnp.bfloat16))
    return low.astype(jnp.float32)

def reference(queries, keys, values, gain, out_grad):
    nblk = TOKENS // BLOCK
    shape4 = (nblk, BLOCK, H, HD)
    qb = queries.reshape(shape4).astype(jnp.float32)
    kb = keys.reshape(shape4).astype(jnp.float32)
    vb = values.reshape(shape4).astype(jnp.float32)
    causal = jnp.tril(jnp.ones((BLOCK, BLOCK), dtype=bool))
    local_kv = jnp.einsum('nshi,nshj->nhij', kb, vb)
    before = jnp.cumsum(local_kv, axis=0)[:-1]
    states = round_half(jnp.concatenate([jnp.zeros_like(local_kv[:1]), before], axis=0))

    def forward_block(pieces):
        qx, kx, vx, sx = pieces
        scores = round_half(jnp.where(causal, jnp.einsum('thi,shi->hts', qx, kx), 0.0))
        return jnp.einsum('hts,shj->thj', scores, vx) + jnp.einsum('thi,hij->thj', qx, sx)
    attended = lax.map(forward_block, (qb, kb, vb, states))
    gains = gain.reshape(H, HD)
    ssq = lax.optimization_barrier(jnp.sum(attended * attended, axis=(2, 3)))
    rinv = lax.rsqrt(ssq / F + 1e-06)[:, :, None, None]
    normed = (attended * rinv * gains).astype(jnp.bfloat16).reshape(TOKENS, F)
    upstream = gains * out_grad.reshape(shape4).astype(jnp.float32)
    mdot = lax.optimization_barrier(jnp.sum(attended * upstream, axis=(2, 3)))[:, :, None, None]
    d_att = round_half(rinv * upstream - attended * rinv ** 3 * mdot / F)
    query_dot = jnp.einsum('nthi,nthj->nhij', qb, d_att)
    later = jnp.cumsum(query_dot[::-1], axis=0)[::-1][1:]
    adjoint = round_half(jnp.concatenate([later, jnp.zeros_like(query_dot[:1])], axis=0))

    def backward_block(pieces):
        qx, kx, vx, dx, sx, gx = pieces
        scores = round_half(jnp.where(causal, jnp.einsum('thi,shi->hts', qx, kx), 0.0))
        back = round_half(jnp.where(causal, jnp.einsum('thj,shj->hts', dx, vx), 0.0))
        grad_q = jnp.einsum('hts,shi->thi', back, kx) + jnp.einsum('thj,hij->thi', dx, sx)
        grad_k = jnp.einsum('hts,thi->shi', back, qx) + jnp.einsum('shj,hij->shi', vx, gx)
        grad_v = jnp.einsum('hts,thj->shj', scores, dx) + jnp.einsum('shi,hij->shj', kx, gx)
        return (grad_q, grad_k, grad_v)
    grad_q, grad_k, grad_v = lax.map(backward_block, (qb, kb, vb, d_att, states, adjoint))
    query_grad = grad_q.astype(jnp.bfloat16).reshape(TOKENS, F)
    key_grad = grad_k.astype(jnp.bfloat16).reshape(TOKENS, F)
    value_grad = grad_v.astype(jnp.bfloat16).reshape(TOKENS, F)
    return (normed, query_grad, key_grad, value_grad)
```

```python
import functools

import jax
import jax.numpy as jnp
from jax import lax
from jax.experimental import pallas as pl
from jax.experimental.pallas import tpu as pltpu
from jax.sharding import PartitionSpec as P

HD = 128
ROWS = 512
HEADS = 4
NY = 4
NZ = 16
NC = NY * NZ
NH = 8
FEATURES = 4096.0
MESH = pl.DeviceIdType.MESH
F32 = jnp.float32
BF16 = jnp.bfloat16


def dot(a, b, ca, cb):
    return lax.dot_general(a, b, (((ca,), (cb,)), ((), ())), preferred_element_type=F32)


def cols(h):
    return slice(h * HD, (h + 1) * HD)


def each_ctx_peer(y, z, visit):
    def turn(k, c):
        half = (k + 1) // 2
        dz = 8 + half * (1 - 2 * (k % 2))
        zz = (z + dz) % NZ
        for dy in (2, 1, 3, 0):
            visit(((y + dy) % NY) * NZ + zz)
        return c

    lax.fori_loop(0, NZ - 1, turn, 0)
    for dy in (2, 1, 3):
        visit(((y + dy) % NY) * NZ + z)


def each_head_peer(head, visit):
    for d in (4, 5, 3, 2, 6, 7, 1):
        visit((head + d) % NH)


def kernel(
    q_ref, k_ref, v_ref, gain_ref, g_ref,
    normed_ref, qg_ref, kg_ref, vg_ref,
    own, gathered, prefix, carry, scores, att, kgi, vgi, datt, norms, norms_in,
    send_sem, recv_sem, norm_send, norm_recv,
):
    ctx = lax.axis_index("ctx")
    head = lax.axis_index("head")
    y, z = ctx // NZ, ctx % NZ

    barrier = pltpu.get_barrier_semaphore()

    def greet(peer):
        pl.semaphore_signal(barrier, inc=1, device_id={"ctx": peer}, device_id_type=MESH)

    def greet_head(peer):
        pl.semaphore_signal(barrier, inc=1, device_id={"head": peer}, device_id_type=MESH)

    each_ctx_peer(y, z, greet)
    each_head_peer(head, greet_head)

    row = lax.broadcasted_iota(jnp.int32, (ROWS, ROWS), 0)
    col = lax.broadcasted_iota(jnp.int32, (ROWS, ROWS), 1)
    causal = row >= col

    def exchange(phase, src, dst, by_peer):
        def send(peer):
            pltpu.make_async_remote_copy(
                src_ref=src.at[phase // 2, peer],
                dst_ref=dst.at[phase // 2, ctx],
                send_sem=send_sem.at[phase],
                recv_sem=recv_sem.at[phase],
                device_id={"ctx": peer},
                device_id_type=MESH,
            ).start()

        each_ctx_peer(y, z, send)

    def arrived(phase, dst):
        view = dst.at[phase // 2, pl.ds(0, NC - 1)]
        pltpu.make_async_copy(view, view, recv_sem.at[phase]).wait()

    def sent(phase, src):
        view = src.at[phase // 2, pl.ds(0, NC - 1)]
        pltpu.make_async_copy(view, view, send_sem.at[phase]).wait()

    def scan(s, beside_out, beside_back):
        exchange(2 * s, own, gathered, True)
        gathered[s, ctx] = own[s, ctx]
        beside_out()
        arrived(2 * s, gathered)
        total = jnp.zeros((8, HD), F32)
        for t in range(NC) if s == 0 else range(NC - 1, -1, -1):
            prefix[s, t] = total
            total = total + gathered[s, t]
        exchange(2 * s + 1, prefix, carry, False)
        carry[s, ctx] = prefix[s, ctx]
        beside_back()
        arrived(2 * s + 1, carry)

    def state(s, h):
        return carry[s, 16 * h : 16 * (h + 1)].reshape(HD, HD).astype(BF16)

    for h in range(HEADS):
        kv = dot(k_ref[:, cols(h)], v_ref[:, cols(h)], 0, 0)
        own[0, 16 * h : 16 * (h + 1)] = kv.reshape(16, 8, HD)

    pl.semaphore_wait(barrier, NC - 1 + NH - 1)

    def forward_intra():
        for h in range(HEADS):
            c = cols(h)
            s = jnp.where(causal, dot(q_ref[:, c], k_ref[:, c], 1, 1), 0.0).astype(BF16)
            scores[h] = s
            att[:, c] = dot(s, v_ref[:, c], 1, 0)

    scan(0, forward_intra, lambda: None)

    ssq = jnp.zeros((ROWS, HD), F32)
    mdot = jnp.zeros((ROWS, HD), F32)
    for h in range(HEADS):
        c = cols(h)
        a = att[:, c] + dot(q_ref[:, c], state(0, h), 1, 0)
        att[:, c] = a
        u = g_ref[:, c].astype(F32) * gain_ref[:, c]
        ssq = ssq + a * a
        mdot = mdot + a * u
    ssq = jnp.sum(ssq, axis=1, keepdims=True)
    mdot = jnp.sum(mdot, axis=1, keepdims=True)
    lane = lax.broadcasted_iota(jnp.int32, (ROWS, HD), 1)
    both = jnp.where(lane < 4, ssq, mdot)
    mine = both.T[0:8]
    norms[...] = mine

    def send_norms(peer):
        pltpu.make_async_remote_copy(
            src_ref=norms,
            dst_ref=norms_in.at[head],
            send_sem=norm_send,
            recv_sem=norm_recv,
            device_id={"head": peer},
            device_id_type=MESH,
        ).start()

    each_head_peer(head, send_norms)
    norms_in[head] = mine
    seven = norms_in.at[pl.ds(0, NH - 1)]
    pltpu.make_async_copy(seven, seven, norm_recv).wait()
    total = norms_in[0]
    for t in range(1, NH):
        total = total + norms_in[t]
    rinv = lax.rsqrt(total[0:1] / FEATURES + 1e-6)
    slope = rinv * rinv * rinv * total[4:5] / FEATURES
    rinv = jnp.broadcast_to(rinv, (HD, ROWS)).T
    slope = jnp.broadcast_to(slope, (HD, ROWS)).T

    for h in range(HEADS):
        c = cols(h)
        u = g_ref[:, c].astype(F32) * gain_ref[:, c]
        d = (rinv * u - att[:, c] * slope).astype(BF16)
        datt[:, c] = d
        own[1, 16 * h : 16 * (h + 1)] = dot(q_ref[:, c], d, 0, 0).reshape(16, 8, HD)

    def backward_intra():
        for h in range(HEADS):
            c = cols(h)
            d = datt[:, c]
            normed_ref[:, c] = (att[:, c] * rinv * gain_ref[:, c]).astype(BF16)
            b = jnp.where(causal, dot(d, v_ref[:, c], 1, 1), 0.0).astype(BF16)
            qg_ref[:, c] = (dot(b, k_ref[:, c], 1, 0) + dot(d, state(0, h), 1, 1)).astype(BF16)
            kgi[:, c] = dot(b, q_ref[:, c], 0, 0)
            vgi[:, c] = dot(scores[h], d, 0, 0)

    scan(1, backward_intra, lambda: None)

    for h in range(HEADS):
        c = cols(h)
        adj = state(1, h)
        kg_ref[:, c] = (kgi[:, c] + dot(v_ref[:, c], adj, 1, 1)).astype(BF16)
        vg_ref[:, c] = (vgi[:, c] + dot(k_ref[:, c], adj, 1, 0)).astype(BF16)

    for s in (0, 1):
        sent(2 * s, own)
        sent(2 * s + 1, prefix)
    pltpu.make_async_copy(seven, seven, norm_send).wait()


def body(queries, keys, values, gain, out_grad):
    vmem = pl.BlockSpec(memory_space=pltpu.VMEM)
    out = jax.ShapeDtypeStruct((ROWS, HEADS * HD), BF16)
    wide = (ROWS, HEADS * HD)
    return pl.pallas_call(
        kernel,
        out_shape=(out,) * 4,
        in_specs=[vmem] * 5,
        out_specs=(vmem,) * 4,
        scratch_shapes=[
            pltpu.VMEM((2, NC, 8, HD), F32),
            pltpu.VMEM((2, NC, 8, HD), F32),
            pltpu.VMEM((2, NC, 8, HD), F32),
            pltpu.VMEM((2, NC, 8, HD), F32),
            pltpu.VMEM((HEADS, ROWS, ROWS), BF16),
            pltpu.VMEM(wide, F32),
            pltpu.VMEM(wide, F32),
            pltpu.VMEM(wide, F32),
            pltpu.VMEM(wide, BF16),
            pltpu.VMEM((8, ROWS), F32),
            pltpu.VMEM((NH, 8, ROWS), F32),
            pltpu.SemaphoreType.DMA((4,)),
            pltpu.SemaphoreType.DMA((4,)),
            pltpu.SemaphoreType.DMA,
            pltpu.SemaphoreType.DMA,
        ],
        compiler_params=pltpu.CompilerParams(
            collective_id=0, has_side_effects=True, vmem_limit_bytes=48 * 2**20
        ),
        name="linear_attention",
    )(queries, keys, values, gain.reshape(1, HEADS * HD), out_grad)


def solution(mesh):
    spec = P("ctx", "head")
    return jax.shard_map(
        body,
        mesh=mesh,
        in_specs=(spec, spec, spec, P("head"), spec),
        out_specs=(spec,) * 4,
        check_vma=False,
    )
```

```python
import functools

import jax
import jax.numpy as jnp
from jax import lax
from jax.experimental import pallas as pl
from jax.experimental.pallas import tpu as pltpu
from jax.sharding import PartitionSpec as P

HD = 128
ROWS = 512
HEADS = 4
NY = 4
NZ = 16
REACH = 4
WINDOW = 2 * REACH
TILES = NY * WINDOW
TILE = HD // TILES
NEIGHBOURS = TILES - 1 + NY + 1
NH = 8
FEATURES = 4096.0
PIECES = 2
MESH = pl.DeviceIdType.MESH
F32 = jnp.float32
BF16 = jnp.bfloat16


def dot(a, b, ca, cb):
    return lax.dot_general(a, b, (((ca,), (cb,)), ((), ())), preferred_element_type=F32)


def cols(h):
    return slice(h * HD, (h + 1) * HD)


def each_in_window(y, z, sign, visit):
    def turn(k, c):
        dz = jnp.where(k % 2 == 0, REACH - k // 2, k // 2 - (REACH - 1)) * sign
        for dy in (2, 1, 3, 0):
            visit((y + dy) % NY, (z + dz + NZ) % NZ)
        return c

    lax.fori_loop(0, 2 * REACH - 1, turn, 0)
    for dy in (2, 1, 3):
        visit((y + dy) % NY, z)


def each_neighbour(y, z, visit):
    each_in_window(y, z, 1, visit)
    for dy in (2, 1, 3, 0):
        visit((y + dy) % NY, (z + NZ - REACH) % NZ)
    visit(y, (z + NZ // 2) % NZ)


def tile_of(y, z):
    return y * WINDOW + z % WINDOW


def each_head_peer(head, visit):
    for d in (4, 5, 3, 2, 6, 7, 1):
        visit((head + d) % NH)


def kernel(
    q_hbm, k_hbm, v_hbm, gain_hbm, g_hbm,
    normed_hbm, qg_hbm, kg_hbm, vg_hbm,
    q_ref, k_ref, v_ref, gain_ref, g_ref, normed_ref, qg_ref, kg_ref, vg_ref,
    own, gathered, rows_out, rows_in, sums, carry, scores, att, kgi, vgi, datt, norms, norms_in,
    load_sem, store_sem, out_send, out_recv, row_send, row_recv, back_send, back_recv,
    norm_send, norm_recv,
):
    ctx = lax.axis_index("ctx")
    head = lax.axis_index("head")
    y, z = ctx // NZ, ctx % NZ
    mine = tile_of(y, z)

    loads = [
        pltpu.make_async_copy(src, dst, load_sem.at[i])
        for i, (src, dst) in enumerate(
            ((k_hbm, k_ref), (v_hbm, v_ref), (q_hbm, q_ref), (g_hbm, g_ref), (gain_hbm, gain_ref))
        )
    ]
    for load in loads:
        load.start()

    barrier = pltpu.get_barrier_semaphore()

    def greet(py, pz):
        pl.semaphore_signal(
            barrier, inc=1, device_id={"ctx": py * NZ + pz}, device_id_type=MESH
        )

    def greet_head(peer):
        pl.semaphore_signal(barrier, inc=1, device_id={"head": peer}, device_id_type=MESH)

    each_neighbour(y, z, greet)
    each_head_peer(head, greet_head)

    row = lax.broadcasted_iota(jnp.int32, (ROWS, ROWS), 0)
    col = lax.broadcasted_iota(jnp.int32, (ROWS, ROWS), 1)
    causal = row >= col

    member = [(z + j + NZ - REACH) % NZ for j in range(WINDOW)]
    wraps = jnp.logical_or(z < REACH, z > NZ - REACH)
    other = (z + NZ // 2) % NZ
    other_wraps = jnp.logical_or(other < REACH, other > NZ - REACH)

    def send_out(s, h):
        def send(py, pz):
            pltpu.make_async_remote_copy(
                src_ref=own.at[s, h, tile_of(py, pz)],
                dst_ref=gathered.at[s, h, y * WINDOW + (z - pz + REACH + NZ) % NZ],
                send_sem=out_send.at[s, h],
                recv_sem=out_recv.at[s, h],
                device_id={"ctx": py * NZ + pz},
                device_id_type=MESH,
            ).start()

        each_in_window(y, z, 1, send)

    def row_copy(s, h):
        return pltpu.make_async_remote_copy(
            src_ref=rows_out.at[s, h],
            dst_ref=rows_in.at[s, h],
            send_sem=row_send.at[s, h],
            recv_sem=row_recv.at[s, h],
            device_id={"ctx": y * NZ + other},
            device_id_type=MESH,
        )

    def add_window(s, h):
        gathered[s, h, y * WINDOW + REACH] = own[s, h, mine]
        view = gathered.at[s, h, pl.ds(0, TILES - 1)]
        pltpu.make_async_copy(view, view, out_recv.at[s, h]).wait()
        zero = jnp.zeros((TILE, HD), F32)
        order = range(WINDOW) if s == 0 else range(WINDOW - 1, -1, -1)
        before = zero
        for r in range(NY):
            at = (r if s == 0 else NY - 1 - r) * WINDOW
            first, whole = zero, zero
            for j in order:
                value = gathered[s, h, at + j]
                leads = member[j] < REACH * 2 if s == 0 else member[j] >= REACH * 2
                first = first + jnp.where(leads, value, 0.0)
                whole = whole + value
            rows_out[s, h, r] = before + jnp.where(wraps, first, whole)
            running = zero
            for j in order:
                leads = member[j] < REACH * 2 if s == 0 else member[j] >= REACH * 2
                start = member[j] == (0 if s == 0 else NZ - 1)
                running = jnp.where(start, 0.0, running)
                extra = jnp.where(jnp.logical_and(wraps, jnp.logical_not(leads)), first, 0.0)
                sums[s, h, at + j] = before + extra + running
                running = running + gathered[s, h, at + j]
            before = before + whole
        row_copy(s, h).start()

    def send_back(s, h):
        view = rows_in.at[s, h]
        pltpu.make_async_copy(view, view, row_recv.at[s, h]).wait()
        for j in range(WINDOW):
            passed = other < member[j] if s == 0 else other > member[j]
            passed = jnp.logical_or(passed, other_wraps)
            for r in range(NY):
                at = (r if s == 0 else NY - 1 - r) * WINDOW + j
                prior = rows_in[s, h, r - 1] if r else jnp.zeros((TILE, HD), F32)
                sums[s, h, at] = sums[s, h, at] + jnp.where(passed, rows_in[s, h, r], prior)

        def send(py, pz):
            pltpu.make_async_remote_copy(
                src_ref=sums.at[s, h, py * WINDOW + (pz - z + REACH + NZ) % NZ],
                dst_ref=carry.at[s, h, mine],
                send_sem=back_send.at[s, h],
                recv_sem=back_recv.at[s, h],
                device_id={"ctx": py * NZ + pz},
                device_id_type=MESH,
            ).start()

        each_in_window(y, z, -1, send)
        pltpu.make_async_copy(
            sums.at[s, h, y * WINDOW + REACH], carry.at[s, h, mine], back_recv.at[s, h]
        ).start()

    def arrived(s, h):
        view = carry.at[s, h]
        pltpu.make_async_copy(view, view, back_recv.at[s, h]).wait()

    def add_up(s):
        for h in range(HEADS):
            add_window(s, h)
        for h in range(HEADS):
            send_back(s, h)

    def state(s, h):
        return carry[s, h].reshape(HD, HD).astype(BF16)

    def store(i, src, dst, c):
        return pltpu.make_async_copy(src.at[:, c], dst.at[:, c], store_sem.at[i])

    loads[0].wait()
    loads[1].wait()
    for h in range(HEADS):
        kv = dot(k_ref[:, cols(h)], v_ref[:, cols(h)], 0, 0)
        own[0, h] = kv.reshape(TILES, TILE, HD)
        if h == 0:
            pl.semaphore_wait(barrier, NEIGHBOURS + NH - 1)
        send_out(0, h)

    for load in loads[2:]:
        load.wait()
    for h in range(HEADS):
        c = cols(h)
        s = jnp.where(causal, dot(q_ref[:, c], k_ref[:, c], 1, 1), 0.0).astype(BF16)
        scores[h] = s
        att[:, c] = dot(s, v_ref[:, c], 1, 0)

    add_up(0)

    ssq = jnp.zeros((ROWS, HD), F32)
    mdot = jnp.zeros((ROWS, HD), F32)
    for h in range(HEADS):
        arrived(0, h)
        c = cols(h)
        a = att[:, c] + dot(q_ref[:, c], state(0, h), 1, 0)
        att[:, c] = a
        u = g_ref[:, c].astype(F32) * gain_ref[:, c]
        ssq = ssq + a * a
        mdot = mdot + a * u
    ssq = jnp.sum(ssq, axis=1, keepdims=True)
    mdot = jnp.sum(mdot, axis=1, keepdims=True)
    lane = lax.broadcasted_iota(jnp.int32, (ROWS, HD), 1)
    flat = jnp.where(lane < 4, ssq, mdot).T[0:8]
    line = lax.broadcasted_iota(jnp.int32, (8, HD), 0) % 4
    packed = flat[:, 0:HD]
    for b in range(1, 4):
        packed = jnp.where(line == b, flat[:, b * HD : (b + 1) * HD], packed)
    norms[...] = packed

    def send_norms(peer):
        pltpu.make_async_remote_copy(
            src_ref=norms,
            dst_ref=norms_in.at[head],
            send_sem=norm_send,
            recv_sem=norm_recv,
            device_id={"head": peer},
            device_id_type=MESH,
        ).start()

    each_head_peer(head, send_norms)
    norms_in[head] = packed
    seven = norms_in.at[pl.ds(0, NH - 1)]
    pltpu.make_async_copy(seven, seven, norm_recv).wait()
    total = norms_in[0]
    for t in range(1, NH):
        total = total + norms_in[t]
    inv = lax.rsqrt(total[0:4] / FEATURES + 1e-6)
    slp = inv * inv * inv * total[4:8] / FEATURES

    def column(x):
        return jnp.concatenate(
            [jnp.broadcast_to(x[b : b + 1], (HD, HD)).T for b in range(4)], axis=0
        )

    rinv = column(inv)
    slope = column(slp)

    for h in range(HEADS):
        c = cols(h)
        u = g_ref[:, c].astype(F32) * gain_ref[:, c]
        d = (rinv * u - att[:, c] * slope).astype(BF16)
        datt[:, c] = d
        own[1, h] = dot(q_ref[:, c], d, 0, 0).reshape(TILES, TILE, HD)
        send_out(1, h)

    for h in range(HEADS):
        c = cols(h)
        d = datt[:, c]
        normed_ref[:, c] = (att[:, c] * rinv * gain_ref[:, c]).astype(BF16)
        b = jnp.where(causal, dot(d, v_ref[:, c], 1, 1), 0.0).astype(BF16)
        qg_ref[:, c] = (dot(b, k_ref[:, c], 1, 0) + dot(d, state(0, h), 1, 1)).astype(BF16)
        kgi[:, c] = dot(b, q_ref[:, c], 0, 0)
        vgi[:, c] = dot(scores[h], d, 0, 0)

    stores = [
        store(i, src, dst, slice(None))
        for i, (src, dst) in enumerate(((normed_ref, normed_hbm), (qg_ref, qg_hbm)))
    ]
    for copy in stores:
        copy.start()

    add_up(1)

    for h in range(HEADS):
        arrived(1, h)
        c = cols(h)
        adj = state(1, h)
        kg_ref[:, c] = (kgi[:, c] + dot(v_ref[:, c], adj, 1, 1)).astype(BF16)
        vg_ref[:, c] = (vgi[:, c] + dot(k_ref[:, c], adj, 1, 0)).astype(BF16)
        for i, (src, dst) in enumerate(((kg_ref, kg_hbm), (vg_ref, vg_hbm))):
            stores.append(store(2 + 2 * h + i, src, dst, c))
            stores[-1].start()

    for s in range(2):
        for h in range(HEADS):
            view = own.at[s, h, pl.ds(0, TILES - 1)]
            pltpu.make_async_copy(view, view, out_send.at[s, h]).wait()
            pltpu.make_async_copy(view, view, back_send.at[s, h]).wait()
            row_copy(s, h).wait_send()
    pltpu.make_async_copy(seven, seven, norm_send).wait()
    for copy in stores:
        copy.wait()


def write_out(a, b, c, d, a_out, b_out, c_out, d_out, held, in_sem, out_sem):
    step = ROWS // PIECES
    loads, stores = [], []
    for i, (src, dst) in enumerate(((a, a_out), (b, b_out), (c, c_out), (d, d_out))):
        for j in range(PIECES):
            rows = pl.ds(j * step, step)
            at = PIECES * i + j
            loads.append(pltpu.make_async_copy(src.at[rows], held.at[i, rows], in_sem.at[at]))
            stores.append(pltpu.make_async_copy(held.at[i, rows], dst.at[rows], out_sem.at[at]))
    for load in loads:
        load.start()
    for load, store in zip(loads, stores):
        load.wait()
        store.start()
    for store in stores:
        store.wait()


def body(queries, keys, values, gain, out_grad):
    hbm = pl.BlockSpec(memory_space=pltpu.HBM)
    out = jax.ShapeDtypeStruct((ROWS, HEADS * HD), BF16)
    wide = (ROWS, HEADS * HD)
    results = pl.pallas_call(
        kernel,
        out_shape=(out,) * 4,
        in_specs=[hbm] * 5,
        out_specs=(hbm,) * 4,
        scratch_shapes=[
            pltpu.VMEM(wide, BF16),
            pltpu.VMEM(wide, BF16),
            pltpu.VMEM(wide, BF16),
            pltpu.VMEM((1, HEADS * HD), F32),
            pltpu.VMEM(wide, BF16),
            pltpu.VMEM(wide, BF16),
            pltpu.VMEM(wide, BF16),
            pltpu.VMEM(wide, BF16),
            pltpu.VMEM(wide, BF16),
            pltpu.VMEM((2, HEADS, TILES, TILE, HD), F32),
            pltpu.VMEM((2, HEADS, TILES, TILE, HD), F32),
            pltpu.VMEM((2, HEADS, NY, TILE, HD), F32),
            pltpu.VMEM((2, HEADS, NY, TILE, HD), F32),
            pltpu.VMEM((2, HEADS, TILES, TILE, HD), F32),
            pltpu.VMEM((2, HEADS, TILES, TILE, HD), F32),
            pltpu.VMEM((HEADS, ROWS, ROWS), BF16),
            pltpu.VMEM(wide, F32),
            pltpu.VMEM(wide, F32),
            pltpu.VMEM(wide, F32),
            pltpu.VMEM(wide, BF16),
            pltpu.VMEM((8, HD), F32),
            pltpu.VMEM((NH, 8, HD), F32),
            pltpu.SemaphoreType.DMA((5,)),
            pltpu.SemaphoreType.DMA((2 + 2 * HEADS,)),
        ]
        + [pltpu.SemaphoreType.DMA((2, HEADS))] * 6
        + [
            pltpu.SemaphoreType.DMA,
            pltpu.SemaphoreType.DMA,
        ],
        compiler_params=pltpu.CompilerParams(
            collective_id=0, has_side_effects=True, vmem_limit_bytes=62 * 2**20
        ),
        name="linear_attention",
    )(queries, keys, values, gain.reshape(1, HEADS * HD), out_grad)
    return pl.pallas_call(
        write_out,
        out_shape=(out,) * 4,
        in_specs=[hbm] * 4,
        out_specs=(hbm,) * 4,
        scratch_shapes=[
            pltpu.VMEM((4,) + wide, BF16),
            pltpu.SemaphoreType.DMA((4 * PIECES,)),
            pltpu.SemaphoreType.DMA((4 * PIECES,)),
        ],
        name="write_out",
    )(*results)


def solution(mesh):
    spec = P("ctx", "head")
    return jax.shard_map(
        body,
        mesh=mesh,
        in_specs=(spec, spec, spec, P("head"), spec),
        out_specs=(spec,) * 4,
        check_vma=False,
    )
```

```python
import functools

import jax
import jax.numpy as jnp
from jax import lax
from jax.experimental import pallas as pl
from jax.experimental.pallas import tpu as pltpu
from jax.sharding import PartitionSpec as P

HD = 128
ROWS = 512
HEADS = 4
NY = 4
NZ = 16
REACH = 4
WINDOW = 2 * REACH
TILES = NY * WINDOW
TILE = HD // TILES
NEIGHBOURS = TILES - 1 + NY + 1
NH = 8
FEATURES = 4096.0
PIECES = 2
MESH = pl.DeviceIdType.MESH
F32 = jnp.float32
BF16 = jnp.bfloat16


def dot(a, b, ca, cb):
    return lax.dot_general(a, b, (((ca,), (cb,)), ((), ())), preferred_element_type=F32)


def cols(h):
    return slice(h * HD, (h + 1) * HD)


def wrap(i, n):
    return lax.rem(i, n)


def each_in_window(y, z, sign, visit):
    def turn(k, c):
        half, odd = lax.div(k, 2), lax.rem(k, 2)
        dz = (REACH - half + odd * (2 * half - 2 * REACH + 1)) * sign
        for dy in (2, 1, 3, 0):
            visit(wrap(y + dy, NY), wrap(z + dz + NZ, NZ))
        return c

    lax.fori_loop(0, 2 * REACH - 1, turn, 0)
    for dy in (2, 1, 3):
        visit(wrap(y + dy, NY), z)


def side(z):
    return 1 - 2 * lax.rem(z, 2)


def below(z):
    return REACH - lax.rem(z, 2)


def each_neighbour(y, z, visit):
    each_in_window(y, z, 1, visit)
    for dy in (2, 1, 3, 0):
        visit(wrap(y + dy, NY), wrap(z + NZ - REACH, NZ))
    visit(y, wrap(z + NZ // 2, NZ))


def tile_of(y, z):
    return y * WINDOW + wrap(z, WINDOW)


def each_head_peer(head, visit):
    for d in (4, 5, 3, 2, 6, 7, 1):
        visit(wrap(head + d, NH))


def kernel(
    q_hbm, k_hbm, v_hbm, gain_hbm, g_hbm,
    normed_hbm, qg_hbm, kg_hbm, vg_hbm,
    q_ref, k_ref, v_ref, gain_ref, g_ref, normed_ref, qg_ref, kg_ref, vg_ref,
    own, gathered, rows_out, rows_in, sums, carry, scores, att, kgi, vgi, datt, norms, norms_in,
    load_sem, store_sem, out_send, out_recv, row_send, row_recv, back_send, back_recv,
    norm_send, norm_recv,
):
    ctx = lax.axis_index("ctx")
    head = lax.axis_index("head")
    y, z = lax.div(ctx, NZ), lax.rem(ctx, NZ)
    mine = tile_of(y, z)

    loads = [
        pltpu.make_async_copy(src, dst, load_sem.at[i])
        for i, (src, dst) in enumerate(
            ((k_hbm, k_ref), (v_hbm, v_ref), (q_hbm, q_ref), (g_hbm, g_ref), (gain_hbm, gain_ref))
        )
    ]
    for load in loads:
        load.start()

    barrier = pltpu.get_barrier_semaphore()

    def greet(py, pz):
        pl.semaphore_signal(
            barrier, inc=1, device_id={"ctx": py * NZ + pz}, device_id_type=MESH
        )

    def greet_head(peer):
        pl.semaphore_signal(barrier, inc=1, device_id={"head": peer}, device_id_type=MESH)

    each_neighbour(y, z, greet)
    each_head_peer(head, greet_head)

    row = lax.broadcasted_iota(jnp.int32, (ROWS, ROWS), 0)
    col = lax.broadcasted_iota(jnp.int32, (ROWS, ROWS), 1)
    causal = row >= col

    low = below(z)
    member = [wrap(z + j + NZ - low, NZ) for j in range(WINDOW)]
    wraps = jnp.logical_or(z < low, z > WINDOW + low)
    other = wrap(z + NZ // 2, NZ)
    other_wraps = jnp.logical_or(other < low, other > WINDOW + low)

    def send_out(s, h):
        def send(py, pz):
            pltpu.make_async_remote_copy(
                src_ref=own.at[s, h, tile_of(py, pz)],
                dst_ref=gathered.at[s, h, y * WINDOW + wrap(z - pz + below(pz) + NZ, NZ)],
                send_sem=out_send.at[s, h],
                recv_sem=out_recv.at[s, h],
                device_id={"ctx": py * NZ + pz},
                device_id_type=MESH,
            ).start()

        each_in_window(y, z, side(z), send)

    def row_copy(s, h):
        return pltpu.make_async_remote_copy(
            src_ref=rows_out.at[s, h],
            dst_ref=rows_in.at[s, h],
            send_sem=row_send.at[s, h],
            recv_sem=row_recv.at[s, h],
            device_id={"ctx": y * NZ + other},
            device_id_type=MESH,
        )

    def add_window(s, h):
        gathered[s, h, y * WINDOW + low] = own[s, h, mine]
        view = gathered.at[s, h, pl.ds(0, TILES - 1)]
        pltpu.make_async_copy(view, view, out_recv.at[s, h]).wait()
        zero = jnp.zeros((TILE, HD), F32)
        order = range(WINDOW) if s == 0 else range(WINDOW - 1, -1, -1)
        before = zero
        for r in range(NY):
            at = (r if s == 0 else NY - 1 - r) * WINDOW
            first, whole = zero, zero
            for j in order:
                value = gathered[s, h, at + j]
                leads = member[j] < REACH * 2 if s == 0 else member[j] >= REACH * 2
                first = first + jnp.where(leads, value, 0.0)
                whole = whole + value
            rows_out[s, h, r] = before + jnp.where(wraps, first, whole)
            running = zero
            for j in order:
                leads = member[j] < REACH * 2 if s == 0 else member[j] >= REACH * 2
                start = member[j] == (0 if s == 0 else NZ - 1)
                running = jnp.where(start, 0.0, running)
                extra = jnp.where(jnp.logical_and(wraps, jnp.logical_not(leads)), first, 0.0)
                sums[s, h, at + j] = before + extra + running
                running = running + gathered[s, h, at + j]
            before = before + whole
        row_copy(s, h).start()

    def send_back(s, h):
        view = rows_in.at[s, h]
        pltpu.make_async_copy(view, view, row_recv.at[s, h]).wait()
        for j in range(WINDOW):
            passed = other < member[j] if s == 0 else other > member[j]
            passed = jnp.logical_or(passed, other_wraps)
            for r in range(NY):
                at = (r if s == 0 else NY - 1 - r) * WINDOW + j
                prior = rows_in[s, h, r - 1] if r else jnp.zeros((TILE, HD), F32)
                sums[s, h, at] = sums[s, h, at] + jnp.where(passed, rows_in[s, h, r], prior)

        def send(py, pz):
            pltpu.make_async_remote_copy(
                src_ref=sums.at[s, h, py * WINDOW + wrap(pz - z + low + NZ, NZ)],
                dst_ref=carry.at[s, h, mine],
                send_sem=back_send.at[s, h],
                recv_sem=back_recv.at[s, h],
                device_id={"ctx": py * NZ + pz},
                device_id_type=MESH,
            ).start()

        each_in_window(y, z, -side(z), send)
        pltpu.make_async_copy(
            sums.at[s, h, y * WINDOW + low], carry.at[s, h, mine], back_recv.at[s, h]
        ).start()

    def arrived(s, h):
        view = carry.at[s, h]
        pltpu.make_async_copy(view, view, back_recv.at[s, h]).wait()

    def add_up(s):
        for h in range(HEADS):
            add_window(s, h)
        for h in range(HEADS):
            send_back(s, h)

    def state(s, h):
        return carry[s, h].reshape(HD, HD).astype(BF16)

    def store(i, src, dst, c):
        return pltpu.make_async_copy(src.at[:, c], dst.at[:, c], store_sem.at[i])

    loads[0].wait()
    loads[1].wait()
    for h in range(HEADS):
        kv = dot(k_ref[:, cols(h)], v_ref[:, cols(h)], 0, 0)
        own[0, h] = kv.reshape(TILES, TILE, HD)
        if h == 0:
            pl.semaphore_wait(barrier, NEIGHBOURS + NH - 1)
        send_out(0, h)

    for load in loads[2:]:
        load.wait()
    for h in range(HEADS):
        c = cols(h)
        s = jnp.where(causal, dot(q_ref[:, c], k_ref[:, c], 1, 1), 0.0).astype(BF16)
        scores[h] = s
        att[:, c] = dot(s, v_ref[:, c], 1, 0)

    add_up(0)

    ssq = jnp.zeros((ROWS, HD), F32)
    mdot = jnp.zeros((ROWS, HD), F32)
    for h in range(HEADS):
        arrived(0, h)
        c = cols(h)
        a = att[:, c] + dot(q_ref[:, c], state(0, h), 1, 0)
        att[:, c] = a
        u = g_ref[:, c].astype(F32) * gain_ref[:, c]
        ssq = ssq + a * a
        mdot = mdot + a * u
    ssq = jnp.sum(ssq, axis=1, keepdims=True)
    mdot = jnp.sum(mdot, axis=1, keepdims=True)
    lane = lax.broadcasted_iota(jnp.int32, (ROWS, HD), 1)
    flat = jnp.where(lane < 4, ssq, mdot).T[0:8]
    line = lax.broadcasted_iota(jnp.int32, (8, HD), 0) % 4
    packed = flat[:, 0:HD]
    for b in range(1, 4):
        packed = jnp.where(line == b, flat[:, b * HD : (b + 1) * HD], packed)
    norms[...] = packed

    def send_norms(peer):
        pltpu.make_async_remote_copy(
            src_ref=norms,
            dst_ref=norms_in.at[head],
            send_sem=norm_send,
            recv_sem=norm_recv,
            device_id={"head": peer},
            device_id_type=MESH,
        ).start()

    each_head_peer(head, send_norms)
    norms_in[head] = packed
    seven = norms_in.at[pl.ds(0, NH - 1)]
    pltpu.make_async_copy(seven, seven, norm_recv).wait()
    total = norms_in[0]
    for t in range(1, NH):
        total = total + norms_in[t]
    inv = lax.rsqrt(total[0:4] / FEATURES + 1e-6)
    slp = inv * inv * inv * total[4:8] / FEATURES

    def column(x):
        return jnp.concatenate(
            [jnp.broadcast_to(x[b : b + 1], (HD, HD)).T for b in range(4)], axis=0
        )

    rinv = column(inv)
    slope = column(slp)

    for h in range(HEADS):
        c = cols(h)
        u = g_ref[:, c].astype(F32) * gain_ref[:, c]
        d = (rinv * u - att[:, c] * slope).astype(BF16)
        datt[:, c] = d
        own[1, h] = dot(q_ref[:, c], d, 0, 0).reshape(TILES, TILE, HD)
        send_out(1, h)

    for h in range(HEADS):
        c = cols(h)
        d = datt[:, c]
        normed_ref[:, c] = (att[:, c] * rinv * gain_ref[:, c]).astype(BF16)
        b = jnp.where(causal, dot(d, v_ref[:, c], 1, 1), 0.0).astype(BF16)
        qg_ref[:, c] = (dot(b, k_ref[:, c], 1, 0) + dot(d, state(0, h), 1, 1)).astype(BF16)
        kgi[:, c] = dot(b, q_ref[:, c], 0, 0)
        vgi[:, c] = dot(scores[h], d, 0, 0)

    stores = [
        store(i, src, dst, slice(None))
        for i, (src, dst) in enumerate(((normed_ref, normed_hbm), (qg_ref, qg_hbm)))
    ]
    for copy in stores:
        copy.start()

    add_up(1)

    for h in range(HEADS):
        arrived(1, h)
        c = cols(h)
        adj = state(1, h)
        kg_ref[:, c] = (kgi[:, c] + dot(v_ref[:, c], adj, 1, 1)).astype(BF16)
        vg_ref[:, c] = (vgi[:, c] + dot(k_ref[:, c], adj, 1, 0)).astype(BF16)
        for i, (src, dst) in enumerate(((kg_ref, kg_hbm), (vg_ref, vg_hbm))):
            stores.append(store(2 + 2 * h + i, src, dst, c))
            stores[-1].start()

    for s in range(2):
        for h in range(HEADS):
            view = own.at[s, h, pl.ds(0, TILES - 1)]
            pltpu.make_async_copy(view, view, out_send.at[s, h]).wait()
            pltpu.make_async_copy(view, view, back_send.at[s, h]).wait()
            row_copy(s, h).wait_send()
    pltpu.make_async_copy(seven, seven, norm_send).wait()
    for copy in stores:
        copy.wait()


def write_out(a, b, c, d, a_out, b_out, c_out, d_out, held, in_sem, out_sem):
    step = ROWS // PIECES
    loads, stores = [], []
    for i, (src, dst) in enumerate(((a, a_out), (b, b_out), (c, c_out), (d, d_out))):
        for j in range(PIECES):
            rows = pl.ds(j * step, step)
            at = PIECES * i + j
            loads.append(pltpu.make_async_copy(src.at[rows], held.at[i, rows], in_sem.at[at]))
            stores.append(pltpu.make_async_copy(held.at[i, rows], dst.at[rows], out_sem.at[at]))
    for load in loads:
        load.start()
    for load, store in zip(loads, stores):
        load.wait()
        store.start()
    for store in stores:
        store.wait()


def body(queries, keys, values, gain, out_grad):
    hbm = pl.BlockSpec(memory_space=pltpu.HBM)
    out = jax.ShapeDtypeStruct((ROWS, HEADS * HD), BF16)
    wide = (ROWS, HEADS * HD)
    results = pl.pallas_call(
        kernel,
        out_shape=(out,) * 4,
        in_specs=[hbm] * 5,
        out_specs=(hbm,) * 4,
        scratch_shapes=[
            pltpu.VMEM(wide, BF16),
            pltpu.VMEM(wide, BF16),
            pltpu.VMEM(wide, BF16),
            pltpu.VMEM((1, HEADS * HD), F32),
            pltpu.VMEM(wide, BF16),
            pltpu.VMEM(wide, BF16),
            pltpu.VMEM(wide, BF16),
            pltpu.VMEM(wide, BF16),
            pltpu.VMEM(wide, BF16),
            pltpu.VMEM((2, HEADS, TILES, TILE, HD), F32),
            pltpu.VMEM((2, HEADS, TILES, TILE, HD), F32),
            pltpu.VMEM((2, HEADS, NY, TILE, HD), F32),
            pltpu.VMEM((2, HEADS, NY, TILE, HD), F32),
            pltpu.VMEM((2, HEADS, TILES, TILE, HD), F32),
            pltpu.VMEM((2, HEADS, TILES, TILE, HD), F32),
            pltpu.VMEM((HEADS, ROWS, ROWS), BF16),
            pltpu.VMEM(wide, F32),
            pltpu.VMEM(wide, F32),
            pltpu.VMEM(wide, F32),
            pltpu.VMEM(wide, BF16),
            pltpu.VMEM((8, HD), F32),
            pltpu.VMEM((NH, 8, HD), F32),
            pltpu.SemaphoreType.DMA((5,)),
            pltpu.SemaphoreType.DMA((2 + 2 * HEADS,)),
        ]
        + [pltpu.SemaphoreType.DMA((2, HEADS))] * 6
        + [
            pltpu.SemaphoreType.DMA,
            pltpu.SemaphoreType.DMA,
        ],
        compiler_params=pltpu.CompilerParams(
            collective_id=0, has_side_effects=True, vmem_limit_bytes=62 * 2**20
        ),
        name="linear_attention",
    )(queries, keys, values, gain.reshape(1, HEADS * HD), out_grad)
    return pl.pallas_call(
        write_out,
        out_shape=(out,) * 4,
        in_specs=[hbm] * 4,
        out_specs=(hbm,) * 4,
        scratch_shapes=[
            pltpu.VMEM((4,) + wide, BF16),
            pltpu.SemaphoreType.DMA((4 * PIECES,)),
            pltpu.SemaphoreType.DMA((4 * PIECES,)),
        ],
        name="write_out",
    )(*results)


def solution(mesh):
    spec = P("ctx", "head")
    return jax.shard_map(
        body,
        mesh=mesh,
        in_specs=(spec, spec, spec, P("head"), spec),
        out_specs=(spec,) * 4,
        check_vma=False,
    )
```

```python
import functools

import jax
import jax.numpy as jnp
from jax import lax
from jax.experimental import pallas as pl
from jax.experimental.pallas import tpu as pltpu
from jax.sharding import PartitionSpec as P

HD = 128
ROWS = 512
HEADS = 4
NY = 4
NZ = 16
REACH = 4
WINDOW = 2 * REACH
TILES = NY * WINDOW
TILE = HD // TILES
NEIGHBOURS = TILES - 1 + NY
NH = 8
FEATURES = 4096.0
PIECES = 2
MESH = pl.DeviceIdType.MESH
F32 = jnp.float32
BF16 = jnp.bfloat16


def dot(a, b, ca, cb):
    return lax.dot_general(a, b, (((ca,), (cb,)), ((), ())), preferred_element_type=F32)


def cols(h):
    return slice(h * HD, (h + 1) * HD)


def wrap(i, n):
    return lax.rem(i, n)


def each_in_window(y, z, sign, visit):
    def turn(k, c):
        half, odd = lax.div(k, 2), lax.rem(k, 2)
        dz = (REACH - half + odd * (2 * half - 2 * REACH + 1)) * sign
        for dy in (2, 1, 3, 0):
            visit(wrap(y + dy, NY), wrap(z + dz + NZ, NZ))
        return c

    lax.fori_loop(0, 2 * REACH - 1, turn, 0)
    for dy in (2, 1, 3):
        visit(wrap(y + dy, NY), z)


def side(z):
    return 1 - 2 * lax.rem(z, 2)


def below(z):
    return REACH - lax.rem(z, 2)


def each_neighbour(y, z, visit):
    each_in_window(y, z, 1, visit)
    for dy in (2, 1, 3, 0):
        visit(wrap(y + dy, NY), wrap(z + NZ - REACH, NZ))


def tile_of(y, z):
    return y * WINDOW + wrap(z, WINDOW)


def each_head_peer(head, visit):
    for d in (4, 5, 3, 2, 6, 7, 1):
        visit(wrap(head + d, NH))


def kernel(
    q_hbm, k_hbm, v_hbm, gain_hbm, g_hbm,
    normed_hbm, qg_hbm, kg_hbm, vg_hbm,
    q_ref, k_ref, v_ref, gain_ref, g_ref, normed_ref, qg_ref, kg_ref, vg_ref,
    own, gathered, rows_out, rows_in, sums, carry, scores, att, kgi, vgi, datt, norms, norms_in,
    load_sem, store_sem, out_send, out_recv, row_send, row_recv, back_send, back_recv,
    norm_send, norm_recv,
):
    ctx = lax.axis_index("ctx")
    head = lax.axis_index("head")
    y, z = lax.div(ctx, NZ), lax.rem(ctx, NZ)
    mine = tile_of(y, z)
    core = lax.rem(head, 2)
    home_head = head + 1 - core

    loads = [
        pltpu.make_async_copy(src, dst, load_sem.at[i])
        for i, (src, dst) in enumerate(
            ((k_hbm, k_ref), (v_hbm, v_ref), (q_hbm, q_ref), (g_hbm, g_ref), (gain_hbm, gain_ref))
        )
    ]
    for load in loads:
        load.start()

    barrier = pltpu.get_barrier_semaphore()

    def greet_at(py, pz, to):
        pl.semaphore_signal(
            barrier, inc=1, device_id={"ctx": py * NZ + pz, "head": to}, device_id_type=MESH
        )

    def greet(py, pz):
        greet_at(py, pz, home_head)
        pl.when(core == 1)(lambda: greet_at(py, pz, head - 1))

    def greet_head(peer):
        pl.semaphore_signal(barrier, inc=1, device_id={"head": peer}, device_id_type=MESH)

    each_neighbour(y, z, greet)
    pl.when(core == 1)(lambda: greet_at(y, wrap(z + NZ // 2, NZ), head))
    each_head_peer(head, greet_head)

    row = lax.broadcasted_iota(jnp.int32, (ROWS, ROWS), 0)
    col = lax.broadcasted_iota(jnp.int32, (ROWS, ROWS), 1)
    causal = row >= col

    low = below(z)
    member = [wrap(z + j + NZ - low, NZ) for j in range(WINDOW)]
    wraps = jnp.logical_or(z < low, z > WINDOW + low)
    other = wrap(z + NZ // 2, NZ)
    other_wraps = jnp.logical_or(other < low, other > WINDOW + low)

    def send_out(s, h):
        def send(py, pz):
            pltpu.make_async_remote_copy(
                src_ref=own.at[s, h, tile_of(py, pz)],
                dst_ref=gathered.at[s, core, h, y * WINDOW + wrap(z - pz + below(pz) + NZ, NZ)],
                send_sem=out_send.at[s, h],
                recv_sem=out_recv.at[s, core, h],
                device_id={"ctx": py * NZ + pz, "head": home_head},
                device_id_type=MESH,
            ).start()

        each_in_window(y, z, side(z), send)
        pl.when(core == 0)(lambda: send(y, z))

    def row_copy(s, c, h):
        return pltpu.make_async_remote_copy(
            src_ref=rows_out.at[s, c, h],
            dst_ref=rows_in.at[s, c, h],
            send_sem=row_send.at[s, c, h],
            recv_sem=row_recv.at[s, c, h],
            device_id={"ctx": y * NZ + other},
            device_id_type=MESH,
        )

    def add_window(s, c, h):
        if c == 1:
            gathered[s, c, h, y * WINDOW + low] = own[s, h, mine]
        view = gathered.at[s, c, h, pl.ds(0, TILES - c)]
        pltpu.make_async_copy(view, view, out_recv.at[s, c, h]).wait()
        zero = jnp.zeros((TILE, HD), F32)
        order = range(WINDOW) if s == 0 else range(WINDOW - 1, -1, -1)
        before = zero
        for r in range(NY):
            at = (r if s == 0 else NY - 1 - r) * WINDOW
            first, whole = zero, zero
            for j in order:
                value = gathered[s, c, h, at + j]
                leads = member[j] < REACH * 2 if s == 0 else member[j] >= REACH * 2
                first = first + jnp.where(leads, value, 0.0)
                whole = whole + value
            rows_out[s, c, h, r] = before + jnp.where(wraps, first, whole)
            running = zero
            for j in order:
                leads = member[j] < REACH * 2 if s == 0 else member[j] >= REACH * 2
                start = member[j] == (0 if s == 0 else NZ - 1)
                running = jnp.where(start, 0.0, running)
                extra = jnp.where(jnp.logical_and(wraps, jnp.logical_not(leads)), first, 0.0)
                sums[s, c, h, at + j] = before + extra + running
                running = running + gathered[s, c, h, at + j]
            before = before + whole
        row_copy(s, c, h).start()

    def send_back(s, c, h):
        view = rows_in.at[s, c, h]
        pltpu.make_async_copy(view, view, row_recv.at[s, c, h]).wait()
        for j in range(WINDOW):
            passed = other < member[j] if s == 0 else other > member[j]
            passed = jnp.logical_or(passed, other_wraps)
            for r in range(NY):
                at = (r if s == 0 else NY - 1 - r) * WINDOW + j
                prior = rows_in[s, c, h, r - 1] if r else jnp.zeros((TILE, HD), F32)
                sums[s, c, h, at] = sums[s, c, h, at] + jnp.where(passed, rows_in[s, c, h, r], prior)

        def send(py, pz):
            pltpu.make_async_remote_copy(
                src_ref=sums.at[s, c, h, py * WINDOW + wrap(pz - z + low + NZ, NZ)],
                dst_ref=carry.at[s, h, mine],
                send_sem=back_send.at[s, c, h],
                recv_sem=back_recv.at[s, h],
                device_id={"ctx": py * NZ + pz, "head": head - 1 + c},
                device_id_type=MESH,
            ).start()

        each_in_window(y, z, -side(z), send)
        if c == 0:
            send(y, z)
        else:
            pltpu.make_async_copy(
                sums.at[s, c, h, y * WINDOW + low], carry.at[s, h, mine], back_recv.at[s, h]
            ).start()

    def arrived(s, h):
        view = carry.at[s, h]
        pltpu.make_async_copy(view, view, back_recv.at[s, h]).wait()

    def add_up(s):
        @pl.when(core == 1)
        def _():
            for h in range(HEADS):
                for c in range(2):
                    add_window(s, c, h)
            for h in range(HEADS):
                for c in range(2):
                    send_back(s, c, h)

    def state(s, h):
        return carry[s, h].reshape(HD, HD).astype(BF16)

    def store(i, src, dst, c):
        return pltpu.make_async_copy(src.at[:, c], dst.at[:, c], store_sem.at[i])

    loads[0].wait()
    loads[1].wait()
    for h in range(HEADS):
        kv = dot(k_ref[:, cols(h)], v_ref[:, cols(h)], 0, 0)
        own[0, h] = kv.reshape(TILES, TILE, HD)
        if h == 0:
            pl.semaphore_wait(barrier, NEIGHBOURS + NH - 1 + core * (NEIGHBOURS + 1))
        send_out(0, h)

    for load in loads[2:]:
        load.wait()
    for h in range(HEADS):
        c = cols(h)
        s = jnp.where(causal, dot(q_ref[:, c], k_ref[:, c], 1, 1), 0.0).astype(BF16)
        scores[h] = s
        att[:, c] = dot(s, v_ref[:, c], 1, 0)

    add_up(0)

    ssq = jnp.zeros((ROWS, HD), F32)
    mdot = jnp.zeros((ROWS, HD), F32)
    for h in range(HEADS):
        arrived(0, h)
        c = cols(h)
        a = att[:, c] + dot(q_ref[:, c], state(0, h), 1, 0)
        att[:, c] = a
        u = g_ref[:, c].astype(F32) * gain_ref[:, c]
        ssq = ssq + a * a
        mdot = mdot + a * u
    ssq = jnp.sum(ssq, axis=1, keepdims=True)
    mdot = jnp.sum(mdot, axis=1, keepdims=True)
    lane = lax.broadcasted_iota(jnp.int32, (ROWS, HD), 1)
    flat = jnp.where(lane < 4, ssq, mdot).T[0:8]
    line = lax.broadcasted_iota(jnp.int32, (8, HD), 0) % 4
    packed = flat[:, 0:HD]
    for b in range(1, 4):
        packed = jnp.where(line == b, flat[:, b * HD : (b + 1) * HD], packed)
    norms[...] = packed

    def send_norms(peer):
        pltpu.make_async_remote_copy(
            src_ref=norms,
            dst_ref=norms_in.at[head],
            send_sem=norm_send,
            recv_sem=norm_recv,
            device_id={"head": peer},
            device_id_type=MESH,
        ).start()

    each_head_peer(head, send_norms)
    norms_in[head] = packed
    seven = norms_in.at[pl.ds(0, NH - 1)]
    pltpu.make_async_copy(seven, seven, norm_recv).wait()
    total = norms_in[0]
    for t in range(1, NH):
        total = total + norms_in[t]
    inv = lax.rsqrt(total[0:4] / FEATURES + 1e-6)
    slp = inv * inv * inv * total[4:8] / FEATURES

    def column(x):
        return jnp.concatenate(
            [jnp.broadcast_to(x[b : b + 1], (HD, HD)).T for b in range(4)], axis=0
        )

    rinv = column(inv)
    slope = column(slp)

    for h in range(HEADS):
        c = cols(h)
        u = g_ref[:, c].astype(F32) * gain_ref[:, c]
        d = (rinv * u - att[:, c] * slope).astype(BF16)
        datt[:, c] = d
        own[1, h] = dot(q_ref[:, c], d, 0, 0).reshape(TILES, TILE, HD)
        send_out(1, h)

    for h in range(HEADS):
        c = cols(h)
        d = datt[:, c]
        normed_ref[:, c] = (att[:, c] * rinv * gain_ref[:, c]).astype(BF16)
        b = jnp.where(causal, dot(d, v_ref[:, c], 1, 1), 0.0).astype(BF16)
        qg_ref[:, c] = (dot(b, k_ref[:, c], 1, 0) + dot(d, state(0, h), 1, 1)).astype(BF16)
        kgi[:, c] = dot(b, q_ref[:, c], 0, 0)
        vgi[:, c] = dot(scores[h], d, 0, 0)

    stores = [
        store(i, src, dst, slice(None))
        for i, (src, dst) in enumerate(((normed_ref, normed_hbm), (qg_ref, qg_hbm)))
    ]
    for copy in stores:
        copy.start()

    add_up(1)

    for h in range(HEADS):
        arrived(1, h)
        c = cols(h)
        adj = state(1, h)
        kg_ref[:, c] = (kgi[:, c] + dot(v_ref[:, c], adj, 1, 1)).astype(BF16)
        vg_ref[:, c] = (vgi[:, c] + dot(k_ref[:, c], adj, 1, 0)).astype(BF16)
        for i, (src, dst) in enumerate(((kg_ref, kg_hbm), (vg_ref, vg_hbm))):
            stores.append(store(2 + 2 * h + i, src, dst, c))
            stores[-1].start()

    def drain(c):
        for s in range(2):
            for h in range(HEADS):
                view = own.at[s, h, pl.ds(0, TILES - c)]
                pltpu.make_async_copy(view, view, out_send.at[s, h]).wait()
                if c == 1:
                    for to in range(2):
                        view = own.at[s, h, pl.ds(0, TILES - to)]
                        pltpu.make_async_copy(view, view, back_send.at[s, to, h]).wait()
                        row_copy(s, to, h).wait_send()

    for c in range(2):
        pl.when(core == c)(functools.partial(drain, c))
    pltpu.make_async_copy(seven, seven, norm_send).wait()
    for copy in stores:
        copy.wait()


def write_out(a, b, c, d, a_out, b_out, c_out, d_out, held, in_sem, out_sem):
    step = ROWS // PIECES
    loads, stores = [], []
    for i, (src, dst) in enumerate(((a, a_out), (b, b_out), (c, c_out), (d, d_out))):
        for j in range(PIECES):
            rows = pl.ds(j * step, step)
            at = PIECES * i + j
            loads.append(pltpu.make_async_copy(src.at[rows], held.at[i, rows], in_sem.at[at]))
            stores.append(pltpu.make_async_copy(held.at[i, rows], dst.at[rows], out_sem.at[at]))
    for load in loads:
        load.start()
    for load, store in zip(loads, stores):
        load.wait()
        store.start()
    for store in stores:
        store.wait()


def body(queries, keys, values, gain, out_grad):
    hbm = pl.BlockSpec(memory_space=pltpu.HBM)
    out = jax.ShapeDtypeStruct((ROWS, HEADS * HD), BF16)
    wide = (ROWS, HEADS * HD)
    results = pl.pallas_call(
        kernel,
        out_shape=(out,) * 4,
        in_specs=[hbm] * 5,
        out_specs=(hbm,) * 4,
        scratch_shapes=[
            pltpu.VMEM(wide, BF16),
            pltpu.VMEM(wide, BF16),
            pltpu.VMEM(wide, BF16),
            pltpu.VMEM((1, HEADS * HD), F32),
            pltpu.VMEM(wide, BF16),
            pltpu.VMEM(wide, BF16),
            pltpu.VMEM(wide, BF16),
            pltpu.VMEM(wide, BF16),
            pltpu.VMEM(wide, BF16),
            pltpu.VMEM((2, HEADS, TILES, TILE, HD), F32),
            pltpu.VMEM((2, 2, HEADS, TILES, TILE, HD), F32),
            pltpu.VMEM((2, 2, HEADS, NY, TILE, HD), F32),
            pltpu.VMEM((2, 2, HEADS, NY, TILE, HD), F32),
            pltpu.VMEM((2, 2, HEADS, TILES, TILE, HD), F32),
            pltpu.VMEM((2, HEADS, TILES, TILE, HD), F32),
            pltpu.VMEM((HEADS, ROWS, ROWS), BF16),
            pltpu.VMEM(wide, F32),
            pltpu.VMEM(wide, F32),
            pltpu.VMEM(wide, F32),
            pltpu.VMEM(wide, BF16),
            pltpu.VMEM((8, HD), F32),
            pltpu.VMEM((NH, 8, HD), F32),
            pltpu.SemaphoreType.DMA((5,)),
            pltpu.SemaphoreType.DMA((2 + 2 * HEADS,)),
        ]
        + [pltpu.SemaphoreType.DMA((2, HEADS))]
        + [pltpu.SemaphoreType.DMA((2, 2, HEADS))] * 4
        + [pltpu.SemaphoreType.DMA((2, HEADS))]
        + [
            pltpu.SemaphoreType.DMA,
            pltpu.SemaphoreType.DMA,
        ],
        compiler_params=pltpu.CompilerParams(
            collective_id=0, has_side_effects=True, vmem_limit_bytes=62 * 2**20
        ),
        name="linear_attention",
    )(queries, keys, values, gain.reshape(1, HEADS * HD), out_grad)
    return pl.pallas_call(
        write_out,
        out_shape=(out,) * 4,
        in_specs=[hbm] * 4,
        out_specs=(hbm,) * 4,
        scratch_shapes=[
            pltpu.VMEM((4,) + wide, BF16),
            pltpu.SemaphoreType.DMA((4 * PIECES,)),
            pltpu.SemaphoreType.DMA((4 * PIECES,)),
        ],
        name="write_out",
    )(*results)


def solution(mesh):
    spec = P("ctx", "head")
    return jax.shard_map(
        body,
        mesh=mesh,
        in_specs=(spec, spec, spec, P("head"), spec),
        out_specs=(spec,) * 4,
        check_vma=False,
    )
```
